256 devices in a mesh: lat: 16 (over y, x), grow: 16 (over z, core).
Axes of the slice: x: 4, y: 4, z: 8, core: 2. Of those that a mesh axis runs over, the one named last changes fastest.
Arguments:
- phase: float32 [256, 512, 512], P('grow', 'lat'), may hold values from -1 to 1
- solute: float32 [256, 512, 512], P('grow', 'lat'), may hold values from -1 to 0.5
- particle: float32 [256, 512, 512], P('grow', 'lat'), may hold values from 0 to 0.6
- inflow: float32 [8, 512, 512], P(None, 'lat'), may hold values from 0.1 to 0.5
Outputs:
- phase_out: float32 [256, 512, 512], P('grow', 'lat')
- solute_out: float32 [256, 512, 512], P('grow', 'lat')
- particle_out: float32 [256, 512, 512], P('grow', 'lat')
The draws below stay inside these ranges and needn't reach their ends.
All inputs are finite; a program needn't handle non-finite values.
Results may differ from the reference program's by a relative error of at most 0.00002.
Values sent between devices are 32-bit elements; how exact they have to be, the bound alone decides.
No kernel may reach another device: no remote copies, remote signals or barrier semaphores. Data moves between devices by JAX's collectives and lax.ppermute only.
A program may use at most 64 MiB of HBM per device.

```python
import jax
import jax.numpy as jnp

NY = 512
STEPS = 2
SHIFT = 8
NZ = 256
NX = 512


def block_levels(rng, extent, cuts, smallest, top_value):
    loudness, own = 1.0, jax.random.fold_in(rng, 6)
    for axis_at, shards_of in cuts:
        steps = jnp.exp(jax.random.uniform(jax.random.fold_in(own, axis_at), (shards_of,), jnp.float32, smallest / len(cuts), top_value / len(cuts)))
        loudness = loudness * jnp.repeat(steps, extent[axis_at] // shards_of).reshape([-1 if axis == axis_at else 1 for axis in range(len(extent))])
    return loudness


def setup_inputs(seed: int = 0) -> dict:
    key_of = jax.random.split(jax.random.key(seed), 5)
    phase = jnp.clip(jax.random.uniform(key_of[0], (NZ, NX, NY), jnp.float32, -1.0, 1.0) * block_levels(key_of[0], (NZ, NX, NY), ((0, 16), (1, 16)), -0.4, 0.0), -1.0, 1.0)
    solute = jnp.clip(-1.0 + 1.5 * jax.random.uniform(key_of[1], (NZ, NX, NY), jnp.float32) ** block_levels(key_of[1], (NZ, NX, NY), ((0, 16), (1, 16)), -0.2, 0.2), -1.0, 0.5)
    particle = jnp.clip(0.6 * jax.random.uniform(key_of[2], (NZ, NX, NY), jnp.float32) ** block_levels(key_of[2], (NZ, NX, NY), ((0, 16), (1, 16)), -0.2, 0.2), 0.0, 0.6)
    inflow = jnp.clip(0.1 + 0.4 * jax.random.uniform(key_of[3], (SHIFT, NX, NY), jnp.float32) ** block_levels(key_of[3], (SHIFT, NX, NY), ((1, 16),), -0.2, 0.2), 0.1, 0.5)
    return {"phase": phase, "solute": solute, "particle": particle, "inflow": inflow}


time_step = 0.09
partition = 0.3
coupling = 2.0
beta_part = 1.0
solute_diff = 0.5
part_diff = 0.3
mobility = 0.5


def neighbours(field):
    centre = field[1:-1, 1:-1]
    return [field[2:, 1:-1], field[:-2, 1:-1], field[1:-1, 2:], field[1:-1, :-2],
            jnp.roll(centre, 1, axis=-1), jnp.roll(centre, -1, axis=-1)]


def advance(grid, height, total):
    phi_all, sol_all, par_all = grid[0], grid[1], grid[2]
    mobile = 0.5 * (1.0 - phi_all)
    carried = par_all * (1.0 - par_all)
    phi_c = phi_all[1:-1, 1:-1]
    sol_c = sol_all[1:-1, 1:-1]
    par_c = par_all[1:-1, 1:-1]
    mob_c = mobile[1:-1, 1:-1]
    car_c = carried[1:-1, 1:-1]
    phi_n = neighbours(phi_all)
    sol_n = neighbours(sol_all)
    par_n = neighbours(par_all)
    mob_n = neighbours(mobile)
    car_n = neighbours(carried)
    laplace = phi_n[0] + phi_n[1] + phi_n[2] + phi_n[3] + phi_n[4] + phi_n[5] - 6.0 * phi_c
    flux_sol = jnp.zeros_like(phi_c)
    flux_par = jnp.zeros_like(phi_c)
    drift = jnp.zeros_like(phi_c)
    for index in range(6):
        face_q = 0.5 * (mob_c + mob_n[index])
        flux_sol = flux_sol + face_q * (sol_n[index] - sol_c)
        flux_par = flux_par + face_q * (par_n[index] - par_c)
        drift = drift + 0.5 * (car_c + car_n[index]) * (phi_n[index] - phi_c)
    theta = (height - 0.5 * total) / total
    lag = 1.0 - (1.0 - partition) * theta
    well = (1.0 - phi_c * phi_c) * (1.0 - phi_c * phi_c)
    rate_phi = (laplace + phi_c - phi_c * phi_c * phi_c
                - coupling * well * (sol_c + theta + beta_part * par_c)) / lag
    weight = 0.5 * (1.0 + partition) - 0.5 * (1.0 - partition) * phi_c
    rate_sol = (solute_diff * flux_sol + 0.5 * (1.0 + (1.0 - partition) * sol_c) * rate_phi) / weight
    rate_par = part_diff * flux_par + mobility * drift
    return jnp.stack([phi_c + time_step * rate_phi, sol_c + time_step * rate_sol,
                      par_c + time_step * rate_par])


def reference(phase, solute, particle, inflow):
    state = jnp.stack([phase, solute, particle])
    height = jnp.arange(NZ, dtype=jnp.float32)[:, None, None]
    for step in range(STEPS):
        grid = jnp.pad(state, ((0, 0), (1, 1), (0, 0), (0, 0)), mode="edge")
        grid = jnp.pad(grid, ((0, 0), (0, 0), (1, 1), (0, 0)), mode="wrap")
        state = advance(grid, height, float(NZ))
    minus = jnp.full((SHIFT, NX, NY), -1.0, dtype=jnp.float32)
    fill = jnp.stack([minus, minus, inflow])
    state = jnp.concatenate([state[:, SHIFT:], fill], axis=1)
    return state[0], state[1], state[2]
```

```python
import functools

import jax
import jax.numpy as jnp
from jax import lax
from jax.experimental import pallas as pl
from jax.experimental.pallas import tpu as pltpu
from jax.sharding import PartitionSpec as P

STEPS = 2
SHIFT = 8

DT = 0.09
PART = 0.3
DU = 0.5
DP = 0.3
MOB = 0.5
ALPHA = DT * DP / 4.0
MU = DT * MOB / 2.0

HALO = STEPS
ROWS = 32
EXT = ROWS + 8
TILES = EXT // 8
FAR = SHIFT + HALO


def tile(t):
    return pl.ds(8 * t, 8)


def extend(base, i, t, s, u, p):
    scaled = ALPHA * p
    carried = p * (MU - MU * p)
    base[i, 3, tile(t)] = scaled + carried
    base[i, 4, tile(t)] = s * (scaled - carried)
    base[i, 5, tile(t)] = s * u


def put(base, i, t, s, u, p):
    base[i, 0, tile(t)] = s
    base[i, 1, tile(t)] = u
    base[i, 2, tile(t)] = p
    extend(base, i, t, s, u, p)


def around(base, i, f, t, sub):
    c = base[i, f, tile(t)]
    before = base[i, f, tile((t - 1) % TILES)]
    after = base[i, f, tile((t + 1) % TILES)]
    n = base[i - 1, f, tile(t)] + base[i + 1, f, tile(t)]
    n = n + pltpu.roll(jnp.where(sub == 7, before, c), 1, 0)
    n = n + pltpu.roll(jnp.where(sub == 0, after, c), 7, 0)
    n = n + pltpu.roll(c, 1, 1)
    n = n + pltpu.roll(c, c.shape[1] - 1, 1)
    return c, n


def advance(base, i, t, sub, theta, gain):
    s, ns = around(base, i, 0, t, sub)
    u, nu = around(base, i, 1, t, sub)
    p = base[i, 2, tile(t)]
    g, ng = around(base, i, 3, t, sub)
    sh, nsh = around(base, i, 4, t, sub)
    su, nsu = around(base, i, 5, t, sub)
    phi = 1.0 - s
    hump = 1.0 - phi * phi
    drive = (u + p) + theta
    rise = ((6.0 * s - ns) + hump * (phi - (hump * drive) * 2.0)) * gain
    flux = (s * nu + nsu) - (u * ns + 6.0 * su)
    weight = PART + (0.5 * (1.0 - PART)) * s
    source = (DT * DU / 4.0) * flux + (0.5 + (0.5 * (1.0 - PART)) * u) * rise
    u_new = u + source * pltpu.reciprocal(weight, full_range=False)
    p_new = p + ((s * ng + nsh) - (g * ns + 6.0 * sh))
    return phi + rise, u_new, p_new


def segment(own, last, start, n_new, total, planes, *refs):
    refs = list(refs)
    take = lambda n: [refs.pop(0) for _ in range(n)]
    if own:
        fields = take(3)
    else:
        (far,) = take(1)
    left, right = take(2)
    if not own:
        (kept, inflow), _ = take(2), take(3)
    outs = take(3)
    if not last:
        (keep,) = take(1)
    raw, sides, base0, base1, res, in_sem, out_sem, keep_sem = take(8)
    old = 0 if own else 2
    n_in = n_new + old
    n_mid = n_in - 2 if own else n_new + 2
    n_out = n_mid - 2
    mid = start + 1 if own else start - 1
    out0 = mid + 1
    if not own:
        fill, kept_vmem = take(2)
    grow = lax.axis_index("grow")
    is_top = grow == lax.axis_size("grow") - 1
    sub = lax.broadcasted_iota(jnp.int32, (8, raw.shape[-1]), 0)

    copies = []
    if not own:
        k = pltpu.make_async_copy(kept, kept_vmem, keep_sem.at[0])
        k.start()
    for f in range(3):
        src = fields[f].at[pl.ds(start, n_new)] if own else far.at[f]
        copies.append(pltpu.make_async_copy(src, raw.at[f], in_sem.at[f]))
    copies.append(pltpu.make_async_copy(left, sides.at[0], in_sem.at[3]))
    copies.append(pltpu.make_async_copy(right, sides.at[1], in_sem.at[4]))
    for c in copies:
        c.start()
    if not own:
        first_fill = max(0, planes - out0)
        n_fill = n_out - first_fill
        f = pltpu.make_async_copy(
            inflow.at[pl.ds(out0 + first_fill - planes, n_fill)], fill.at[pl.ds(first_fill, n_fill)], in_sem.at[5]
        )
        f.start()
        k.wait()

        def revive(i, _):
            for which, base in ((0, base0), (1, base1)):
                for t in range(TILES):
                    s, u, p = (kept_vmem[which, i, f, tile(t)] for f in range(3))
                    put(base, i, t, s, u, p)
            return 0

        lax.fori_loop(0, 2, revive, 0)
    for c in copies:
        c.wait()

    def load(i, _):
        for t in range(ROWS // 8):
            phi, u, p = (raw[f, i, tile(t)] for f in range(3))
            put(base0, i + old, t, 1.0 - phi, u, p)
        edge = []
        for f in range(3):
            low, high = sides[0, f, i], sides[1, f, i]
            edge.append(jnp.concatenate([high, jnp.zeros((4, high.shape[1]), jnp.float32), low], axis=0))
        put(base0, i + old, TILES - 1, 1.0 - edge[0], edge[1], edge[2])
        return 0

    lax.fori_loop(0, n_new, load, 0)

    above = planes - start
    if not own and 0 <= above < n_in:

        @pl.when(is_top)
        def _():
            base0[above] = base0[above - 1]

    def coefficients(plane):
        height = (grow * planes + plane).astype(jnp.float32)
        theta = (height - 0.5 * total) / total
        lag = jnp.full(sub.shape, 1.0 - (1.0 - PART) * theta, jnp.float32)
        return theta, DT / lag

    def middle(i, _):
        at = i + 1 if own else i - 1
        theta, gain = coefficients(mid + i)
        for t in range(TILES):
            phi, u, p = advance(base0, at, t, sub, theta, gain)
            put(base1, i, t, 1.0 - phi, u, p)
        return 0

    lax.fori_loop(0 if own else 2, n_mid, middle, 0)

    above = planes - mid
    if not own and 0 <= above < n_mid:

        @pl.when(is_top)
        def _():
            base1[above] = base1[above - 1]

    keeping = []
    if not last:
        for which, base, n in ((0, base0, n_in), (1, base1, n_mid)):
            keeping.append(
                pltpu.make_async_copy(base.at[pl.ds(n - 2, 2), pl.ds(0, 3)], keep.at[which], keep_sem.at[1 + which])
            )
        for c in keeping:
            c.start()

    def write(i):
        return [
            pltpu.make_async_copy(res.at[f, i], outs[f].at[out0 - SHIFT + i], out_sem.at[f, i]) for f in range(3)
        ]

    if not own:
        f.wait()

    def final(i, _):
        theta, gain = coefficients(out0 + i)
        for t in range(ROWS // 8):
            phi, u, p = advance(base1, i + 1, t, sub, theta, gain)
            res[0, i, tile(t)] = phi
            res[1, i, tile(t)] = u
            res[2, i, tile(t)] = p
        if not own:

            @pl.when(jnp.logical_and(is_top, out0 + i >= planes))
            def _():
                res[0, i] = jnp.full(res.shape[2:], -1.0, jnp.float32)
                res[1, i] = jnp.full(res.shape[2:], -1.0, jnp.float32)
                res[2, i] = fill[i]

        for c in write(i):
            c.start()
        return 0

    lax.fori_loop(0, n_out, final, 0)

    def finish(i, _):
        for c in write(i):
            c.wait()
        return 0

    lax.fori_loop(0, n_out, finish, 0)
    for c in keeping:
        c.wait()


def run(own, last, start, n_new, total, planes, shape, ins, outs=None):
    ny = shape[2]
    old = 0 if own else 2
    n_in = n_new + old
    n_mid = n_in - 2 if own else n_new + 2
    n_out = n_mid - 2
    any_ = pl.BlockSpec(memory_space=pl.ANY)
    f32 = jnp.float32
    out_shape = [jax.ShapeDtypeStruct(shape, f32)] * 3
    if not last:
        out_shape.append(jax.ShapeDtypeStruct((2, 2, 3, EXT, ny), f32))
    scratch = [
        pltpu.VMEM((3, n_new, ROWS, ny), f32),
        pltpu.VMEM((2, 3, n_new, HALO, ny), f32),
        pltpu.VMEM((n_in, 6, EXT, ny), f32),
        pltpu.VMEM((n_mid, 6, EXT, ny), f32),
        pltpu.VMEM((3, n_out, ROWS, ny), f32),
        pltpu.SemaphoreType.DMA((6,)),
        pltpu.SemaphoreType.DMA((3, n_out)),
        pltpu.SemaphoreType.DMA((3,)),
    ]
    if not own:
        scratch += [pltpu.VMEM((n_out, ROWS, ny), f32), pltpu.VMEM((2, 2, 3, EXT, ny), f32)]
    args = list(ins) + (list(outs) if outs is not None else [])
    alias = {} if outs is None else {len(ins) + k: k for k in range(3)}
    cells = (n_in * EXT + n_mid * EXT + n_out * ROWS) * ny
    return pl.pallas_call(
        functools.partial(segment, own, last, start, n_new, total, planes),
        out_shape=out_shape,
        in_specs=[any_] * len(args),
        out_specs=[any_] * len(out_shape),
        scratch_shapes=scratch,
        input_output_aliases=alias,
        compiler_params=pltpu.CompilerParams(vmem_limit_bytes=28 << 20),
        cost_estimate=pl.CostEstimate(flops=60 * cells, bytes_accessed=20 * cells, transcendentals=0),
        name="first_run" if own else "last_run" if last else "next_run",
    )(*args)


NEAR = 7


def on_device(phase, solute, particle, inflow):
    planes, rows, ny = phase.shape
    n_lat, n_grow = lax.axis_size("lat"), lax.axis_size("grow")
    total = float(n_grow * planes)
    down = [(i + 1, i) for i in range(n_grow - 1)]
    east = [(i, (i + 1) % n_lat) for i in range(n_lat)]
    west = [((i + 1) % n_lat, i) for i in range(n_lat)]
    fields = (phase, solute, particle)

    def cut(lo, hi, a, b):
        return jnp.stack([f[lo:hi, a:b] for f in fields])

    def diagonal(pairs):
        return [(l * n_grow + g, m * n_grow + h) for l, m in pairs for g, h in down]

    both = ("lat", "grow")
    near = lax.ppermute(cut(0, NEAR, 0, rows), "grow", down)
    lo = planes - SHIFT - HALO
    left = lax.ppermute(cut(lo, planes, rows - HALO, rows), "lat", east)
    right = lax.ppermute(cut(lo, planes, 0, HALO), "lat", west)
    far_left = lax.ppermute(cut(0, FAR, rows - HALO, rows), both, diagonal(east))
    far_right = lax.ppermute(cut(0, FAR, 0, HALO), both, diagonal(west))
    rest = lax.ppermute(cut(NEAR, FAR, 0, rows), "grow", down)

    *outs, keep = run(True, False, lo, planes - lo, total, planes, phase.shape, (*fields, left, right))
    *outs, keep = run(
        False, False, planes - 2, NEAR, total, planes, phase.shape,
        (near, far_left[:, :NEAR], far_right[:, :NEAR], keep, inflow), outs,
    )
    return tuple(
        run(
            False, True, planes - 2 + NEAR, FAR - NEAR, total, planes, phase.shape,
            (rest, far_left[:, NEAR:], far_right[:, NEAR:], keep, inflow), outs,
        )
    )


def solution(mesh):
    in_specs = (
        P("grow", "lat", None),
        P("grow", "lat", None),
        P("grow", "lat", None),
        P(None, "lat", None),
    )
    out_specs = (P("grow", "lat", None), P("grow", "lat", None), P("grow", "lat", None))
    return jax.shard_map(
        on_device, mesh=mesh, in_specs=in_specs, out_specs=out_specs, check_vma=False
    )
```

```python
import functools

import jax
import jax.numpy as jnp
from jax import lax
from jax.experimental import pallas as pl
from jax.experimental.pallas import tpu as pltpu
from jax.sharding import PartitionSpec as P

STEPS = 2
SHIFT = 8

DT = 0.09
PART = 0.3
DU = 0.5
DP = 0.3
MOB = 0.5
ALPHA = DT * DP / 4.0
MU = DT * MOB / 2.0

HALO = STEPS
ROWS = 32
EXT = ROWS + 8
TILES = EXT // 8
FAR = SHIFT + HALO


def tile(t):
    return pl.ds(8 * t, 8)


def put(base, i, t, s, u, p):
    scaled = ALPHA * p
    carried = p * (MU - MU * p)
    base[i, 0, tile(t)] = s
    base[i, 1, tile(t)] = u
    base[i, 2, tile(t)] = p
    base[i, 3, tile(t)] = scaled + carried
    base[i, 4, tile(t)] = s * (scaled - carried)
    base[i, 5, tile(t)] = s * u


def around(base, i, f, t, sub):
    c = base[i, f, tile(t)]
    before = base[i, f, tile((t - 1) % TILES)]
    after = base[i, f, tile((t + 1) % TILES)]
    n = base[i - 1, f, tile(t)] + base[i + 1, f, tile(t)]
    n = n + pltpu.roll(jnp.where(sub == 7, before, c), 1, 0)
    n = n + pltpu.roll(jnp.where(sub == 0, after, c), 7, 0)
    n = n + pltpu.roll(c, 1, 1)
    n = n + pltpu.roll(c, c.shape[1] - 1, 1)
    return c, n


def advance(base, i, t, sub, theta, gain):
    s, ns = around(base, i, 0, t, sub)
    u, nu = around(base, i, 1, t, sub)
    p = base[i, 2, tile(t)]
    g, ng = around(base, i, 3, t, sub)
    sh, nsh = around(base, i, 4, t, sub)
    su, nsu = around(base, i, 5, t, sub)
    phi = 1.0 - s
    hump = 1.0 - phi * phi
    drive = (u + p) + theta
    rise = ((6.0 * s - ns) + hump * (phi - (hump * drive) * 2.0)) * gain
    flux = (s * nu + nsu) - (u * ns + 6.0 * su)
    weight = PART + (0.5 * (1.0 - PART)) * s
    source = (DT * DU / 4.0) * flux + (0.5 + (0.5 * (1.0 - PART)) * u) * rise
    u_new = u + source * pltpu.reciprocal(weight, full_range=False)
    p_new = p + ((s * ng + nsh) - (g * ns + 6.0 * sh))
    return phi + rise, u_new, p_new


def pack(lo, chunks, *refs):
    fields, held, refs = refs[:4], refs[4:8], refs[8:]
    parts, (east, west, sem) = refs[: len(chunks)], refs[len(chunks) :]
    planes = fields[0].shape[0]
    own, lowest = [], []
    for f in range(3):
        own.append(pltpu.make_async_copy(fields[f].at[pl.ds(lo, planes - lo)], held[f], sem.at[f, 0]))
        first, copies = 0, []
        for k, (part, count) in enumerate(zip(parts, chunks)):
            copies.append(pltpu.make_async_copy(fields[f].at[pl.ds(first, count)], part.at[f], sem.at[f, 1 + k]))
            first += count
        lowest.append(copies)
    entering = pltpu.make_async_copy(fields[3], held[3], sem.at[3, 0])
    for f in range(3):
        for c in [own[f], *lowest[f]]:
            c.start()
    entering.start()
    for f in range(3):
        first = 0
        for part, count, c in zip(parts, chunks, lowest[f]):
            c.wait()

            @pl.loop(0, min(count, lo - first))
            def _(i):
                east[f, first + i] = part[f, i, ROWS - HALO : ROWS]
                west[f, first + i] = part[f, i, 0:HALO]

            first += count
        own[f].wait()

        @pl.loop(0, planes - lo)
        def _(i):
            east[f, lo + i] = held[f][i, ROWS - HALO : ROWS]
            west[f, lo + i] = held[f][i, 0:HALO]

    entering.wait()


def pack_sides(left, right, part, _, mixed, __):
    n, t_all = part.shape[1], ROWS // 8

    @pl.loop(0, n)
    def _(i):
        for f in range(3):
            for t in range(t_all):
                mixed[f, t_all * i + t] = part[f, i, tile(t)]

    @pl.loop(0, FAR // 2)
    def _(i):
        for f in range(3):
            rows = [a[f, i + h] for h in (0, FAR // 2) for a in (right, left)]
            mixed[f, t_all * n + i] = jnp.concatenate(rows, axis=0)


def segment(own, tiled, sides, lo, start, n_new, total, planes, *refs):
    refs = list(refs)
    take = lambda n: [refs.pop(0) for _ in range(n)]
    if own:
        fields = take(3)
        left, right = take(2)
    else:
        inner, mixed, inflow = take(3)
        take(5)
    outs = take(3)
    base0, base1 = take(2)
    res, out_sem = take(2)
    grow = lax.axis_index("grow")
    is_top = grow == lax.axis_size("grow") - 1
    sub = lax.broadcasted_iota(jnp.int32, (8, res.shape[-1]), 0)
    mid0 = start + (1 if own else -1)
    out0 = start + (2 if own else -2)
    n_mid, n_out = (n_new - 2, n_new - 4) if own else (n_new, n_new)
    far0 = start - planes

    @pl.loop(0, n_new)
    def _(i):
        for t in range(ROWS // 8):
            if own:
                phi, u, p = (fields[f][i, tile(t)] for f in range(3))
            elif tiled:
                phi, u, p = (inner[f, ROWS // 8 * i + t] for f in range(3))
            else:
                phi, u, p = (inner[f, i, tile(t)] for f in range(3))
            put(base0, start - lo + i, t, 1.0 - phi, u, p)
        ends = []
        for f in range(3):
            if own:
                low, high = left[f, start + i], right[f, start + i]
                ends.append(jnp.concatenate([high, jnp.zeros((4, high.shape[1]), jnp.float32), low], axis=0))
            else:
                upper = far0 + i >= FAR // 2
                both = mixed[f, sides + jnp.where(upper, far0 + i - FAR // 2, far0 + i)]
                ends.append(jnp.where((sub < 4) != upper, both, pltpu.roll(both, 4, 0)))
        put(base0, start - lo + i, TILES - 1, 1.0 - ends[0], ends[1], ends[2])

    def close(base, first, at, n):
        if first <= at < first + n:

            @pl.when(is_top)
            def _():
                base[at] = base[at - 1]

    close(base0, start - lo, planes - lo, n_new)

    def coefficients(plane):
        height = (grow * planes + plane).astype(jnp.float32)
        theta = (height - 0.5 * total) / total
        lag = jnp.full(sub.shape, 1.0 - (1.0 - PART) * theta, jnp.float32)
        return theta, DT / lag

    @pl.loop(0, n_mid)
    def _(i):
        theta, gain = coefficients(mid0 + i)
        for t in range(TILES):
            phi, u, p = advance(base0, mid0 - lo + i, t, sub, theta, gain)
            put(base1, mid0 - lo - 1 + i, t, 1.0 - phi, u, p)

    close(base1, mid0 - lo - 1, planes - lo - 1, n_mid)

    def write(i):
        return [
            pltpu.make_async_copy(res.at[f, i], outs[f].at[out0 - SHIFT + i], out_sem.at[f, i]) for f in range(3)
        ]

    @pl.loop(0, n_out)
    def _(i):
        theta, gain = coefficients(out0 + i)
        for t in range(ROWS // 8):
            phi, u, p = advance(base1, out0 - lo - 1 + i, t, sub, theta, gain)
            res[0, i, tile(t)] = phi
            res[1, i, tile(t)] = u
            res[2, i, tile(t)] = p
        if not own:

            @pl.when(jnp.logical_and(is_top, out0 + i >= planes))
            def _():
                res[0, i] = jnp.full(res.shape[2:], -1.0, jnp.float32)
                res[1, i] = jnp.full(res.shape[2:], -1.0, jnp.float32)
                res[2, i] = inflow[jnp.maximum(out0 - planes + i, 0)]

        for c in write(i):
            c.start()

    @pl.loop(0, n_out)
    def _(i):
        for c in write(i):
            c.wait()


IN_HBM = pl.BlockSpec(memory_space=pltpu.HBM)
IN_VMEM = pl.BlockSpec(memory_space=pltpu.VMEM)
F32 = jnp.float32


def in_vmem(*shape):
    return pltpu.VMEM(shape, F32)


def near_memory(*arrays):
    return [pltpu.with_memory_space_constraint(a, pltpu.VMEM) for a in arrays]


def run(own, tiled, sides, lo, start, n_new, total, planes, shape, ins, outs=None):
    ny = shape[2]
    n_mid, n_out = (n_new - 2, n_new - 4) if own else (n_new, n_new)
    deep = planes - lo + FAR
    out_shape = [jax.ShapeDtypeStruct(shape, F32)] * 3
    out_shape += [in_vmem(deep, 6, EXT, ny), in_vmem(deep - 2, 6, EXT, ny)]
    scratch = [pltpu.VMEM((3, n_out, ROWS, ny), F32), pltpu.SemaphoreType.DMA((3, n_out))]
    alias = {}
    out_specs = [IN_HBM] * 3 + [IN_VMEM] * 2
    args, in_specs = near_memory(*ins), [IN_VMEM] * len(ins)
    if not own:
        alias = {len(args) + k: k for k in range(5)}
        args += list(outs)
        in_specs += [IN_HBM] * 3 + [IN_VMEM] * 2
    cells = (n_new * 10 + n_mid * EXT + n_out * ROWS) * ny
    return pl.pallas_call(
        functools.partial(segment, own, tiled, sides, lo, start, n_new, total, planes),
        out_shape=out_shape,
        in_specs=in_specs,
        out_specs=out_specs,
        scratch_shapes=scratch,
        input_output_aliases=alias,
        compiler_params=pltpu.CompilerParams(vmem_limit_bytes=8 << 20),
        cost_estimate=pl.CostEstimate(flops=COST_FLOPS * cells, bytes_accessed=COST_BYTES * cells, transcendentals=0),
        name="own_run" if own else f"far_run_{start - planes}",
    )(*args)


PACK_LIMIT = 57 << 20
COST_FLOPS, COST_BYTES = 60, 16
CHUNKS = (6, 2, 2)


def on_device(phase, solute, particle, inflow):
    planes, rows, ny = phase.shape
    n_lat, n_grow = lax.axis_size("lat"), lax.axis_size("grow")
    total = float(n_grow * planes)
    down = [(i + 1, i) for i in range(n_grow - 1)]
    to_east = [(i, (i + 1) % n_lat) for i in range(n_lat)]
    to_west = [((i + 1) % n_lat, i) for i in range(n_lat)]
    lo = planes - SHIFT - HALO
    packed = pl.pallas_call(
        functools.partial(pack, lo, CHUNKS),
        out_shape=[in_vmem(planes - lo, rows, ny)] * 3
        + [in_vmem(*inflow.shape)]
        + [in_vmem(3, n, rows, ny) for n in CHUNKS]
        + [in_vmem(3, planes, HALO, ny)] * 2,
        in_specs=[IN_HBM] * 4,
        out_specs=[IN_VMEM] * (6 + len(CHUNKS)),
        scratch_shapes=[pltpu.SemaphoreType.DMA((4, 1 + len(CHUNKS)))],
        compiler_params=pltpu.CompilerParams(vmem_limit_bytes=PACK_LIMIT),
        name="pack",
    )(phase, solute, particle, inflow)
    fields, inflow, (near, more, rest), (east, west) = packed[:3], packed[3], packed[4:-2], packed[-2:]
    near = lax.ppermute(near, "grow", down)
    left = lax.ppermute(east, "lat", to_east)
    right = lax.ppermute(west, "lat", to_west)
    sides = CHUNKS[1] * (rows // 8)
    mixed, rest = pl.pallas_call(
        pack_sides,
        out_shape=[in_vmem(3, sides + FAR // 2, 8, ny), in_vmem(*rest.shape)],
        in_specs=[IN_VMEM] * 4,
        out_specs=[IN_VMEM] * 2,
        input_output_aliases={3: 1},
        compiler_params=pltpu.CompilerParams(vmem_limit_bytes=1 << 20),
        name="pack_sides",
    )(*near_memory(left, right, more, rest))
    mixed = lax.ppermute(mixed, "grow", down)
    rest = lax.ppermute(rest, "grow", down)

    state = run(True, False, 0, lo, lo, planes - lo, total, planes, phase.shape, (*fields, left, right))
    start = planes
    for n, part in zip(CHUNKS, (near, mixed, rest)):
        tiled = part is mixed
        state = run(False, tiled, sides, lo, start, n, total, planes, phase.shape, (part, mixed, inflow), state)
        start += n
    return tuple(state[:3])


def solution(mesh):
    in_specs = (
        P("grow", "lat", None),
        P("grow", "lat", None),
        P("grow", "lat", None),
        P(None, "lat", None),
    )
    out_specs = (P("grow", "lat", None), P("grow", "lat", None), P("grow", "lat", None))
    return jax.shard_map(
        on_device, mesh=mesh, in_specs=in_specs, out_specs=out_specs, check_vma=False
    )
```

```python
import functools

import jax
import jax.numpy as jnp
from jax import lax
from jax.experimental import pallas as pl
from jax.experimental.pallas import tpu as pltpu
from jax.sharding import PartitionSpec as P

STEPS = 2
SHIFT = 8

DT = 0.09
PART = 0.3
DU = 0.5
DP = 0.3
MOB = 0.5
ALPHA = DT * DP / 4.0
MU = DT * MOB / 2.0

HALO = STEPS
ROWS = 32
EXT = ROWS + 8
TILES = EXT // 8
FAR = SHIFT + HALO


def tile(t):
    return pl.ds(8 * t, 8)


def put(base, i, t, s, u, p):
    scaled = ALPHA * p
    carried = p * (MU - MU * p)
    base[i, 0, tile(t)] = s
    base[i, 1, tile(t)] = u
    base[i, 2, tile(t)] = p
    base[i, 3, tile(t)] = scaled + carried
    base[i, 4, tile(t)] = s * (scaled - carried)
    base[i, 5, tile(t)] = s * u


def around(base, i, f, t, sub):
    c = base[i, f, tile(t)]
    before = base[i, f, tile((t - 1) % TILES)]
    after = base[i, f, tile((t + 1) % TILES)]
    n = base[i - 1, f, tile(t)] + base[i + 1, f, tile(t)]
    n = n + pltpu.roll(jnp.where(sub == 7, before, c), 1, 0)
    n = n + pltpu.roll(jnp.where(sub == 0, after, c), 7, 0)
    n = n + pltpu.roll(c, 1, 1)
    n = n + pltpu.roll(c, c.shape[1] - 1, 1)
    return c, n


def advance(base, i, t, sub, theta, gain):
    s, ns = around(base, i, 0, t, sub)
    u, nu = around(base, i, 1, t, sub)
    p = base[i, 2, tile(t)]
    g, ng = around(base, i, 3, t, sub)
    sh, nsh = around(base, i, 4, t, sub)
    su, nsu = around(base, i, 5, t, sub)
    phi = 1.0 - s
    hump = 1.0 - phi * phi
    drive = (u + p) + theta
    rise = ((6.0 * s - ns) + hump * (phi - (hump * drive) * 2.0)) * gain
    flux = (s * nu + nsu) - (u * ns + 6.0 * su)
    weight = PART + (0.5 * (1.0 - PART)) * s
    source = (DT * DU / 4.0) * flux + (0.5 + (0.5 * (1.0 - PART)) * u) * rise
    u_new = u + source * pltpu.reciprocal(weight, full_range=False)
    p_new = p + ((s * ng + nsh) - (g * ns + 6.0 * sh))
    return phi + rise, u_new, p_new


def fetch(phase, solute, particle, near, sem):
    copies = [
        pltpu.make_async_copy(a.at[pl.ds(0, near.shape[1])], near.at[f], sem.at[f])
        for f, a in enumerate((phase, solute, particle))
    ]
    for c in copies:
        c.start()
    for c in copies:
        c.wait()


def pack(lo, chunks, *refs):
    fields, near, held, refs = refs[:4], refs[4], refs[5:9], refs[9:]
    later, (east, west, sem) = refs[: len(chunks) - 1], refs[len(chunks) - 1 :]
    planes = fields[0].shape[0]
    own, lowest = [], []
    for f in range(3):
        own.append(pltpu.make_async_copy(fields[f].at[pl.ds(lo, planes - lo)], held[f], sem.at[f, 0]))
        first, copies = chunks[0], []
        for k, (part, count) in enumerate(zip(later, chunks[1:])):
            copies.append(pltpu.make_async_copy(fields[f].at[pl.ds(first, count)], part.at[f], sem.at[f, 1 + k]))
            first += count
        lowest.append(copies)
    entering = pltpu.make_async_copy(fields[3], held[3], sem.at[3, 0])
    for f in range(3):
        for c in [own[f], *lowest[f]]:
            c.start()
    entering.start()

    @pl.loop(0, min(lo, chunks[0]))
    def _(i):
        for f in range(3):
            east[f, i] = near[f, i, ROWS - HALO : ROWS]
            west[f, i] = near[f, i, 0:HALO]

    for f in range(3):
        own[f].wait()

        @pl.loop(0, planes - lo)
        def _(i):
            east[f, lo + i] = held[f][i, ROWS - HALO : ROWS]
            west[f, lo + i] = held[f][i, 0:HALO]

    for f in range(3):
        for c in lowest[f]:
            c.wait()
    entering.wait()


def pack_sides(left, right, part, _, done, mixed, __):
    n, t_all = part.shape[1], ROWS // 8

    @pl.loop(0, n)
    def _(i):
        for f in range(3):
            for t in range(t_all):
                mixed[f, t_all * i + t] = part[f, i, tile(t)]

    @pl.loop(0, FAR // 2)
    def _(i):
        for f in range(3):
            rows = [a[f, i + h] for h in (0, FAR // 2) for a in (right, left)]
            mixed[f, t_all * n + i] = jnp.concatenate(rows, axis=0)


N_TILES = ROWS // 8


def planewise(n, tiles):
    step = min(n, max(1, 8 // tiles))

    def over(body):
        whole = n // step * step

        @pl.loop(0, whole, step=step)
        def _(i):
            for k in range(step):
                body(i + k)

        for i in range(whole, n):
            body(jnp.int32(i))

    return over


FULL, INNER, OUTER = "full", "inner", "outer"
MIDDLE_TILES = {FULL: range(TILES), INNER: range(N_TILES), OUTER: (0, N_TILES - 1, TILES - 1)}
FINAL_TILES = {FULL: range(N_TILES), INNER: range(1, N_TILES - 1), OUTER: (0, N_TILES - 1)}


def segment(kind, own, tiled, writes, beside, lo, start, n_new, total, planes, ins, outs, base0, base1, res, out_sem):
    ins = list(ins)
    take = lambda n: [ins.pop(0) for _ in range(n)]
    rows_in = kind != OUTER
    sides_in = kind != INNER
    if own:
        if rows_in:
            fields = take(3)
        if sides_in:
            left, right = take(2)
    else:
        if rows_in:
            (inner,) = take(1)
        if sides_in:
            (mixed,) = take(1)
        (inflow,) = take(1)
    grow = lax.axis_index("grow")
    is_top = grow == lax.axis_size("grow") - 1
    sub = lax.broadcasted_iota(jnp.int32, (8, res.shape[-1]), 0)
    mid0 = start + (1 if own else -1)
    out0 = start + (2 if own else -2)
    n_mid, n_out = (n_new - 2, n_new - 4) if own else (n_new, n_new)
    far0 = start - planes

    @pl.loop(0, n_new)
    def _(i):
        for t in range(N_TILES) if rows_in else ():
            if own:
                phi, u, p = (fields[f][i, tile(t)] for f in range(3))
            elif tiled:
                phi, u, p = (inner[f, N_TILES * i + t] for f in range(3))
            else:
                phi, u, p = (inner[f, i, tile(t)] for f in range(3))
            put(base0, start - lo + i, t, 1.0 - phi, u, p)
        ends = []
        for f in range(3) if sides_in else ():
            if own:
                low, high = left[f, start + i], right[f, start + i]
                ends.append(jnp.concatenate([high, jnp.zeros((4, high.shape[1]), jnp.float32), low], axis=0))
            else:
                upper = far0 + i >= FAR // 2
                both = mixed[f, beside + jnp.where(upper, far0 + i - FAR // 2, far0 + i)]
                ends.append(jnp.where((sub < 4) != upper, both, pltpu.roll(both, 4, 0)))
        if sides_in:
            put(base0, start - lo + i, TILES - 1, 1.0 - ends[0], ends[1], ends[2])

    def close(base, first, at, n):
        if first <= at < first + n:

            @pl.when(is_top)
            def _():
                base[at] = base[at - 1]

    close(base0, start - lo, planes - lo, n_new)

    def coefficients(plane):
        height = (grow * planes + plane).astype(jnp.float32)
        theta = (height - 0.5 * total) / total
        lag = jnp.full(sub.shape, 1.0 - (1.0 - PART) * theta, jnp.float32)
        return theta, DT / lag

    @planewise(n_mid, len(MIDDLE_TILES[kind]))
    def _(i):
        theta, gain = coefficients(mid0 + i)
        for t in MIDDLE_TILES[kind]:
            phi, u, p = advance(base0, mid0 - lo + i, t, sub, theta, gain)
            put(base1, mid0 - lo - 1 + i, t, 1.0 - phi, u, p)

    close(base1, mid0 - lo - 1, planes - lo - 1, n_mid)

    def write(i):
        at = out0 - SHIFT + i
        return [pltpu.make_async_copy(res.at[f, at], outs[f].at[at], out_sem.at[f, at]) for f in range(3)]

    @planewise(n_out, len(FINAL_TILES[kind]))
    def _(i):
        theta, gain = coefficients(out0 + i)
        at = out0 - SHIFT + i
        for t in FINAL_TILES[kind]:
            phi, u, p = advance(base1, out0 - lo - 1 + i, t, sub, theta, gain)
            res[0, at, tile(t)] = phi
            res[1, at, tile(t)] = u
            res[2, at, tile(t)] = p
        if kind != INNER and not own:

            @pl.when(jnp.logical_and(is_top, out0 + i >= planes))
            def _():
                res[0, at] = jnp.full(res.shape[2:], -1.0, jnp.float32)
                res[1, at] = jnp.full(res.shape[2:], -1.0, jnp.float32)
                res[2, at] = inflow[jnp.maximum(out0 - planes + i, 0)]

        if writes:
            for c in write(i):
                c.start()

    def finish():
        if writes:

            @pl.loop(0, n_out)
            def _(i):
                for c in write(i):
                    c.wait()

    return finish


def several(parts, ready, n_ins, aliased, *refs):
    ins, refs = refs[:n_ins], refs[n_ins + (6 if aliased else 0) :]
    outs, state, sem = refs[:3], refs[3:6], refs[-1]
    if not aliased:
        refs[6][...] = jnp.zeros_like(refs[6])
    copies = []
    if ready:
        first, run_of = ready[0], pl.ds(*ready)
        for f in range(3):
            copies.append(pltpu.make_async_copy(state[2].at[f, run_of], outs[f].at[run_of], sem.at[f, first]))
    for c in copies:
        c.start()
    waits = [part([ins[k] for k in places], outs, *state, sem) for part, places in parts]
    for c in copies:
        c.wait()
    for wait in waits:
        wait()


IN_HBM = pl.BlockSpec(memory_space=pltpu.HBM)
IN_VMEM = pl.BlockSpec(memory_space=pltpu.VMEM)
F32 = jnp.float32


def in_vmem(*shape):
    return pltpu.VMEM(shape, F32)


def near_memory(*arrays):
    return [pltpu.with_memory_space_constraint(a, pltpu.VMEM) for a in arrays]


def run(name, parts, ins, shape, deep, cost, state=None, ready=None):
    planes, rows, ny = shape
    out_shape = [jax.ShapeDtypeStruct(shape, F32)] * 3
    out_shape += [in_vmem(deep, 6, EXT, ny), in_vmem(deep - 2, 6, EXT, ny), in_vmem(3, *shape)]
    args, in_specs, alias = near_memory(*ins), [IN_VMEM] * len(ins), {}
    out_specs = [IN_HBM] * 3 + [IN_VMEM] * 3
    if state is None:
        out_shape.append(in_vmem(8, 128))
        out_specs.append(IN_VMEM)
    else:
        alias = {len(args) + k: k for k in range(6)}
        args += list(state)
        in_specs += [IN_HBM] * 3 + [IN_VMEM] * 3
    return pl.pallas_call(
        functools.partial(several, parts, ready, len(ins), state is not None),
        out_shape=out_shape,
        in_specs=in_specs,
        out_specs=out_specs,
        scratch_shapes=[pltpu.SemaphoreType.DMA((3, planes))],
        input_output_aliases=alias,
        compiler_params=pltpu.CompilerParams(vmem_limit_bytes=4 << 20),
        cost_estimate=pl.CostEstimate(flops=480 * ny * cost, bytes_accessed=128 * ny * cost, transcendentals=0),
        name=name,
    )(*args)


PACK_LIMIT = 57 << 20
CHUNKS = (7, 1, 2)


def on_device(phase, solute, particle, inflow):
    planes, rows, ny = phase.shape
    n_lat, n_grow = lax.axis_size("lat"), lax.axis_size("grow")
    total = float(n_grow * planes)
    down = [(i + 1, i) for i in range(n_grow - 1)]
    to_east = [(i, (i + 1) % n_lat) for i in range(n_lat)]
    to_west = [((i + 1) % n_lat, i) for i in range(n_lat)]
    lo = planes - SHIFT - HALO
    assert CHUNKS[0] >= lo
    fat = pltpu.CompilerParams(vmem_limit_bytes=PACK_LIMIT)
    near = pl.pallas_call(
        fetch,
        out_shape=in_vmem(3, CHUNKS[0], rows, ny),
        in_specs=[IN_HBM] * 3,
        out_specs=IN_VMEM,
        scratch_shapes=[pltpu.SemaphoreType.DMA((3,))],
        compiler_params=fat,
        name="fetch",
    )(phase, solute, particle)
    packed = pl.pallas_call(
        functools.partial(pack, lo, CHUNKS),
        out_shape=[in_vmem(planes - lo, rows, ny)] * 3
        + [in_vmem(*inflow.shape)]
        + [in_vmem(3, n, rows, ny) for n in CHUNKS[1:]]
        + [in_vmem(3, planes, HALO, ny)] * 2,
        in_specs=[IN_HBM] * 4 + [IN_VMEM],
        out_specs=[IN_VMEM] * (5 + len(CHUNKS)),
        scratch_shapes=[pltpu.SemaphoreType.DMA((4, len(CHUNKS)))],
        compiler_params=fat,
        name="pack",
    )(phase, solute, particle, inflow, *near_memory(near))
    fields, inflow, (more, rest), (east, west) = packed[:3], packed[3], packed[4:-2], packed[-2:]
    near = lax.ppermute(near, "grow", down)
    left = lax.ppermute(east, "lat", to_east)
    right = lax.ppermute(west, "lat", to_west)
    beside = CHUNKS[1] * (rows // 8)

    def part(kind, own, tiled, writes, start, n):
        return functools.partial(segment, kind, own, tiled, writes, beside, lo, start, n, total, planes)

    n, start, deep = CHUNKS, planes, planes - lo + FAR
    own = (lo, planes - lo)
    parts = [(part(INNER, True, False, False, *own), (0, 1, 2))]
    *state, done = run("own_inner", parts, fields, phase.shape, deep, 60)
    mixed, rest = pl.pallas_call(
        pack_sides,
        out_shape=[in_vmem(3, beside + FAR // 2, 8, ny), in_vmem(*rest.shape)],
        in_specs=[IN_VMEM] * 5,
        out_specs=[IN_VMEM] * 2,
        input_output_aliases={3: 1},
        compiler_params=pltpu.CompilerParams(vmem_limit_bytes=1 << 20),
        name="pack_sides",
    )(*near_memory(left, right, more, rest, done))
    mixed = lax.ppermute(mixed, "grow", down)
    rest = lax.ppermute(rest, "grow", down)

    parts = [(part(OUTER, True, False, False, *own), (0, 1))]
    state = run("own_outer", parts, (left, right), phase.shape, deep, 50, state)
    parts = [(part(INNER, False, False, False, start, n[0]), (0, 1))]
    n_own = planes - lo - 2 * HALO
    state = run("near_inner", parts, (near, inflow), phase.shape, deep, 60, state, (0, n_own))
    parts = [
        (part(OUTER, False, False, False, start, n[0]), (0, 1)),
        (part(FULL, False, True, False, start + n[0], n[1]), (0, 0, 1)),
    ]
    state = run("near_outer", parts, (mixed, inflow), phase.shape, deep, 60, state)
    parts = [(part(FULL, False, False, True, start + n[0] + n[1], n[2]), (0, 1, 2))]
    state = run("rest", parts, (rest, mixed, inflow), phase.shape, deep, 20, state, (n_own, n[0] + n[1]))
    return tuple(state[:3])


def solution(mesh):
    in_specs = (
        P("grow", "lat", None),
        P("grow", "lat", None),
        P("grow", "lat", None),
        P(None, "lat", None),
    )
    out_specs = (P("grow", "lat", None), P("grow", "lat", None), P("grow", "lat", None))
    return jax.shard_map(
        on_device, mesh=mesh, in_specs=in_specs, out_specs=out_specs, check_vma=False
    )
```

```python
import functools

import jax
import jax.numpy as jnp
from jax import lax
from jax.experimental import pallas as pl
from jax.experimental.pallas import tpu as pltpu
from jax.sharding import PartitionSpec as P

STEPS = 2
SHIFT = 8

DT = 0.09
PART = 0.3
DU = 0.5
DP = 0.3
MOB = 0.5
ALPHA = DT * DP / 4.0
MU = DT * MOB / 2.0
HALF = 0.5 * (1.0 - PART)

HALO = STEPS
ROWS = 32
EXT = ROWS + 8
TILES = EXT // 8
FAR = SHIFT + HALO


def tile(t):
    return pl.ds(8 * t, 8)


def put(base, i, t, s, u, p):
    m = MU * p
    base[i, 0, tile(t)] = s
    base[i, 1, tile(t)] = u
    base[i, 2, tile(t)] = p
    base[i, 3, tile(t)] = p * ((ALPHA + MU) - m)
    base[i, 4, tile(t)] = s * (p * ((ALPHA - MU) + m))
    base[i, 5, tile(t)] = s * u


def around(base, i, f, t, sub):
    c = base[i, f, tile(t)]
    before = base[i, f, tile((t - 1) % TILES)]
    after = base[i, f, tile((t + 1) % TILES)]
    n = base[i - 1, f, tile(t)] + base[i + 1, f, tile(t)]
    n = n + pltpu.roll(jnp.where(sub == 7, before, c), 1, 0)
    n = n + pltpu.roll(jnp.where(sub == 0, after, c), 7, 0)
    return c, n


def along(c):
    return pltpu.roll(c, 1, 1), pltpu.roll(c, c.shape[1] - 1, 1)


def advance(base, i, t, sub, theta, gain):
    s, ns = around(base, i, 0, t, sub)
    u, nu = around(base, i, 1, t, sub)
    _, nsu = around(base, i, 5, t, sub)
    (s0, s1), (u0, u1) = along(s), along(u)
    ns = ns + s0 + s1
    nu = nu + u0 + u1
    nsu = nsu + s0 * u0 + s1 * u1
    p = base[i, 2, tile(t)]
    g, ng = around(base, i, 3, t, sub)
    sh, nsh = around(base, i, 4, t, sub)
    (g0, g1), (h0, h1) = along(g), along(sh)
    ng = ng + g0 + g1
    nsh = nsh + h0 + h1
    six = 6.0 * s
    phi = 1.0 - s
    hump = 1.0 - phi * phi
    drive = (u + p) + theta
    rise = ((six - ns) + hump * (phi - (hump * drive) * 2.0)) * gain
    flux = (s * nu + nsu) - u * (ns + six)
    source = (DT * DU / 4.0 / HALF) * flux + (0.5 / HALF + u) * rise
    u_new = u + source * pltpu.reciprocal(s + PART / HALF, full_range=False)
    p_new = p + ((s * ng + nsh) - (g * ns + 6.0 * sh))
    return phi, rise, s - rise, u_new, p_new


def fetch(phase, solute, particle, near, sem):
    copies = [
        pltpu.make_async_copy(a.at[pl.ds(0, near.shape[1])], near.at[f], sem.at[f])
        for f, a in enumerate((phase, solute, particle))
    ]
    for c in copies:
        c.start()
    for c in copies:
        c.wait()


def pack(lo, chunks, *refs):
    fields, near, held, refs = refs[:4], refs[4], refs[5:9], refs[9:]
    later, (east, west, sem) = refs[: len(chunks) - 1], refs[len(chunks) - 1 :]
    planes = fields[0].shape[0]
    own, lowest = [], []
    for f in range(3):
        own.append(pltpu.make_async_copy(fields[f].at[pl.ds(lo, planes - lo)], held[f], sem.at[f, 0]))
        first, copies = chunks[0], []
        for k, (part, count) in enumerate(zip(later, chunks[1:])):
            copies.append(pltpu.make_async_copy(fields[f].at[pl.ds(first, count)], part.at[f], sem.at[f, 1 + k]))
            first += count
        lowest.append(copies)
    entering = pltpu.make_async_copy(fields[3], held[3], sem.at[3, 0])
    for f in range(3):
        for c in [own[f], *lowest[f]]:
            c.start()
    entering.start()

    @pl.loop(0, min(lo, chunks[0]))
    def _(i):
        for f in range(3):
            east[f, i] = near[f, i, ROWS - HALO : ROWS]
            west[f, i] = near[f, i, 0:HALO]

    for f in range(3):
        own[f].wait()

        @pl.loop(0, planes - lo)
        def _(i):
            east[f, lo + i] = held[f][i, ROWS - HALO : ROWS]
            west[f, lo + i] = held[f][i, 0:HALO]

    for f in range(3):
        for c in lowest[f]:
            c.wait()
    entering.wait()


def pack_sides(left, right, part, _, done, mixed, __):
    n, t_all = part.shape[1], ROWS // 8

    @pl.loop(0, n)
    def _(i):
        for f in range(3):
            for t in range(t_all):
                mixed[f, t_all * i + t] = part[f, i, tile(t)]

    @pl.loop(0, FAR // 2)
    def _(i):
        for f in range(3):
            rows = [a[f, i + h] for h in (0, FAR // 2) for a in (right, left)]
            mixed[f, t_all * n + i] = jnp.concatenate(rows, axis=0)


N_TILES = ROWS // 8


def planewise(n, tiles):
    step = min(n, max(1, 8 // tiles))

    def over(body):
        whole = n // step * step

        @pl.loop(0, whole, step=step)
        def _(i):
            for k in range(step):
                body(i + k)

        for i in range(whole, n):
            body(jnp.int32(i))

    return over


FULL, INNER, OUTER = "full", "inner", "outer"
MIDDLE_TILES = {FULL: range(TILES), INNER: range(N_TILES), OUTER: (0, N_TILES - 1, TILES - 1)}
FINAL_TILES = {FULL: range(N_TILES), INNER: range(1, N_TILES - 1), OUTER: (0, N_TILES - 1)}


def segment(kind, own, tiled, writes, beside, lo, start, n_new, total, planes, ins, outs, base0, base1, res, out_sem):
    ins = list(ins)
    take = lambda n: [ins.pop(0) for _ in range(n)]
    rows_in = kind != OUTER
    sides_in = kind != INNER
    if own:
        if rows_in:
            fields = take(3)
        if sides_in:
            left, right = take(2)
    else:
        if rows_in:
            (inner,) = take(1)
        if sides_in:
            (mixed,) = take(1)
        (inflow,) = take(1)
    grow = lax.axis_index("grow")
    is_top = grow == lax.axis_size("grow") - 1
    sub = lax.broadcasted_iota(jnp.int32, (8, res.shape[-1]), 0)
    mid0 = start + (1 if own else -1)
    out0 = start + (2 if own else -2)
    n_mid, n_out = (n_new - 2, n_new - 4) if own else (n_new, n_new)
    far0 = start - planes

    @pl.loop(0, n_new)
    def _(i):
        for t in range(N_TILES) if rows_in else ():
            if own:
                phi, u, p = (fields[f][i, tile(t)] for f in range(3))
            elif tiled:
                phi, u, p = (inner[f, N_TILES * i + t] for f in range(3))
            else:
                phi, u, p = (inner[f, i, tile(t)] for f in range(3))
            put(base0, start - lo + i, t, 1.0 - phi, u, p)
        ends = []
        for f in range(3) if sides_in else ():
            if own:
                low, high = left[f, start + i], right[f, start + i]
                ends.append(jnp.concatenate([high, jnp.zeros((4, high.shape[1]), jnp.float32), low], axis=0))
            else:
                upper = far0 + i >= FAR // 2
                both = mixed[f, beside + jnp.where(upper, far0 + i - FAR // 2, far0 + i)]
                ends.append(jnp.where((sub < 4) != upper, both, pltpu.roll(both, 4, 0)))
        if sides_in:
            put(base0, start - lo + i, TILES - 1, 1.0 - ends[0], ends[1], ends[2])

    def close(base, first, at, n):
        if first <= at < first + n:

            @pl.when(is_top)
            def _():
                base[at] = base[at - 1]

    close(base0, start - lo, planes - lo, n_new)

    def coefficients(plane):
        height = (grow * planes + plane).astype(jnp.float32)
        theta = (height - 0.5 * total) / total
        lag = jnp.full(sub.shape, 1.0 - (1.0 - PART) * theta, jnp.float32)
        return theta, DT / lag

    @planewise(n_mid, len(MIDDLE_TILES[kind]))
    def _(i):
        theta, gain = coefficients(mid0 + i)
        for t in MIDDLE_TILES[kind]:
            _, _, s, u, p = advance(base0, mid0 - lo + i, t, sub, theta, gain)
            put(base1, mid0 - lo - 1 + i, t, s, u, p)

    close(base1, mid0 - lo - 1, planes - lo - 1, n_mid)

    def write(i):
        at = out0 - SHIFT + i
        return [pltpu.make_async_copy(res.at[f, at], outs[f].at[at], out_sem.at[f, at]) for f in range(3)]

    @planewise(n_out, len(FINAL_TILES[kind]))
    def _(i):
        theta, gain = coefficients(out0 + i)
        at = out0 - SHIFT + i
        for t in FINAL_TILES[kind]:
            phi, rise, _, u, p = advance(base1, out0 - lo - 1 + i, t, sub, theta, gain)
            res[0, at, tile(t)] = phi + rise
            res[1, at, tile(t)] = u
            res[2, at, tile(t)] = p
        if kind != INNER and not own:

            @pl.when(jnp.logical_and(is_top, out0 + i >= planes))
            def _():
                res[0, at] = jnp.full(res.shape[2:], -1.0, jnp.float32)
                res[1, at] = jnp.full(res.shape[2:], -1.0, jnp.float32)
                res[2, at] = inflow[jnp.maximum(out0 - planes + i, 0)]

        if writes:
            for c in write(i):
                c.start()

    def finish():
        if writes:

            @pl.loop(0, n_out)
            def _(i):
                for c in write(i):
                    c.wait()

    return finish


def several(parts, ready, n_ins, aliased, *refs):
    ins, refs = refs[:n_ins], refs[n_ins + (6 if aliased else 0) :]
    outs, state, sem = refs[:3], refs[3:6], refs[-1]
    if not aliased:
        refs[6][...] = jnp.zeros_like(refs[6])
    copies = []
    if ready:
        first, run_of = ready[0], pl.ds(*ready)
        for f in range(3):
            copies.append(pltpu.make_async_copy(state[2].at[f, run_of], outs[f].at[run_of], sem.at[f, first]))
    for c in copies:
        c.start()
    waits = [part([ins[k] for k in places], outs, *state, sem) for part, places in parts]
    for c in copies:
        c.wait()
    for wait in waits:
        wait()


IN_HBM = pl.BlockSpec(memory_space=pltpu.HBM)
IN_VMEM = pl.BlockSpec(memory_space=pltpu.VMEM)
F32 = jnp.float32


def in_vmem(*shape):
    return pltpu.VMEM(shape, F32)


def near_memory(*arrays):
    return [pltpu.with_memory_space_constraint(a, pltpu.VMEM) for a in arrays]


def run(name, parts, ins, shape, deep, cost, state=None, ready=None):
    planes, rows, ny = shape
    out_shape = [jax.ShapeDtypeStruct(shape, F32)] * 3
    out_shape += [in_vmem(deep, 6, EXT, ny), in_vmem(deep - 2, 6, EXT, ny), in_vmem(3, *shape)]
    args, in_specs, alias = near_memory(*ins), [IN_VMEM] * len(ins), {}
    out_specs = [IN_HBM] * 3 + [IN_VMEM] * 3
    if state is None:
        out_shape.append(in_vmem(8, 128))
        out_specs.append(IN_VMEM)
    else:
        alias = {len(args) + k: k for k in range(6)}
        args += list(state)
        in_specs += [IN_HBM] * 3 + [IN_VMEM] * 3
    return pl.pallas_call(
        functools.partial(several, parts, ready, len(ins), state is not None),
        out_shape=out_shape,
        in_specs=in_specs,
        out_specs=out_specs,
        scratch_shapes=[pltpu.SemaphoreType.DMA((3, planes))],
        input_output_aliases=alias,
        compiler_params=pltpu.CompilerParams(vmem_limit_bytes=4 << 20),
        cost_estimate=pl.CostEstimate(flops=480 * ny * cost, bytes_accessed=128 * ny * cost, transcendentals=0),
        name=name,
    )(*args)


PACK_LIMIT = 57 << 20
CHUNKS = (7, 1, 2)


def on_device(phase, solute, particle, inflow):
    planes, rows, ny = phase.shape
    n_lat, n_grow = lax.axis_size("lat"), lax.axis_size("grow")
    total = float(n_grow * planes)
    down = [(i + 1, i) for i in range(n_grow - 1)]
    to_east = [(i, (i + 1) % n_lat) for i in range(n_lat)]
    to_west = [((i + 1) % n_lat, i) for i in range(n_lat)]
    lo = planes - SHIFT - HALO
    assert CHUNKS[0] >= lo
    fat = pltpu.CompilerParams(vmem_limit_bytes=PACK_LIMIT)
    near = pl.pallas_call(
        fetch,
        out_shape=in_vmem(3, CHUNKS[0], rows, ny),
        in_specs=[IN_HBM] * 3,
        out_specs=IN_VMEM,
        scratch_shapes=[pltpu.SemaphoreType.DMA((3,))],
        compiler_params=fat,
        name="fetch",
    )(phase, solute, particle)
    packed = pl.pallas_call(
        functools.partial(pack, lo, CHUNKS),
        out_shape=[in_vmem(planes - lo, rows, ny)] * 3
        + [in_vmem(*inflow.shape)]
        + [in_vmem(3, n, rows, ny) for n in CHUNKS[1:]]
        + [in_vmem(3, planes, HALO, ny)] * 2,
        in_specs=[IN_HBM] * 4 + [IN_VMEM],
        out_specs=[IN_VMEM] * (5 + len(CHUNKS)),
        scratch_shapes=[pltpu.SemaphoreType.DMA((4, len(CHUNKS)))],
        compiler_params=fat,
        name="pack",
    )(phase, solute, particle, inflow, *near_memory(near))
    fields, inflow, (more, rest), (east, west) = packed[:3], packed[3], packed[4:-2], packed[-2:]
    near = lax.ppermute(near, "grow", down)
    left = lax.ppermute(east, "lat", to_east)
    right = lax.ppermute(west, "lat", to_west)
    beside = CHUNKS[1] * (rows // 8)

    def part(kind, own, tiled, writes, start, n):
        return functools.partial(segment, kind, own, tiled, writes, beside, lo, start, n, total, planes)

    n, start, deep = CHUNKS, planes, planes - lo + FAR
    own = (lo, planes - lo)
    parts = [(part(INNER, True, False, False, *own), (0, 1, 2))]
    *state, done = run("own_inner", parts, fields, phase.shape, deep, 60)
    mixed, rest = pl.pallas_call(
        pack_sides,
        out_shape=[in_vmem(3, beside + FAR // 2, 8, ny), in_vmem(*rest.shape)],
        in_specs=[IN_VMEM] * 5,
        out_specs=[IN_VMEM] * 2,
        input_output_aliases={3: 1},
        compiler_params=pltpu.CompilerParams(vmem_limit_bytes=1 << 20),
        name="pack_sides",
    )(*near_memory(left, right, more, rest, done))
    mixed = lax.ppermute(mixed, "grow", down)
    rest = lax.ppermute(rest, "grow", down)

    parts = [(part(OUTER, True, False, False, *own), (0, 1))]
    state = run("own_outer", parts, (left, right), phase.shape, deep, 50, state)
    parts = [(part(INNER, False, False, False, start, n[0]), (0, 1))]
    n_own = planes - lo - 2 * HALO
    state = run("near_inner", parts, (near, inflow), phase.shape, deep, 60, state, (0, n_own))
    parts = [
        (part(OUTER, False, False, False, start, n[0]), (0, 1)),
        (part(FULL, False, True, False, start + n[0], n[1]), (0, 0, 1)),
    ]
    state = run("near_outer", parts, (mixed, inflow), phase.shape, deep, 60, state)
    parts = [(part(FULL, False, False, True, start + n[0] + n[1], n[2]), (0, 1, 2))]
    state = run("rest", parts, (rest, mixed, inflow), phase.shape, deep, 20, state, (n_own, n[0] + n[1]))
    return tuple(state[:3])


def solution(mesh):
    in_specs = (
        P("grow", "lat", None),
        P("grow", "lat", None),
        P("grow", "lat", None),
        P(None, "lat", None),
    )
    out_specs = (P("grow", "lat", None), P("grow", "lat", None), P("grow", "lat", None))
    return jax.shard_map(
        on_device, mesh=mesh, in_specs=in_specs, out_specs=out_specs, check_vma=False
    )
```

```python
import functools

import jax
import jax.numpy as jnp
from jax import lax
from jax.experimental import pallas as pl
from jax.experimental.pallas import tpu as pltpu
from jax.sharding import PartitionSpec as P

STEPS = 2
SHIFT = 8

DT = 0.09
PART = 0.3
DU = 0.5
DP = 0.3
MOB = 0.5
ALPHA = DT * DP / 4.0
MU = DT * MOB / 2.0
HALF = 0.5 * (1.0 - PART)

HALO = STEPS
ROWS = 32
EXT = ROWS + 8
TILES = EXT // 8
FAR = SHIFT + HALO


def tile(t):
    return pl.ds(8 * t, 8)


def put(base, i, t, s, u, p):
    m = MU * p
    base[i, 0, tile(t)] = s
    base[i, 1, tile(t)] = u
    base[i, 2, tile(t)] = p
    base[i, 3, tile(t)] = p * ((ALPHA + MU) - m)
    base[i, 4, tile(t)] = s * (p * ((ALPHA - MU) + m))
    base[i, 5, tile(t)] = s * u


def around(base, i, f, t, sub):
    c = base[i, f, tile(t)]
    before = base[i, f, tile((t - 1) % TILES)]
    after = base[i, f, tile((t + 1) % TILES)]
    n = base[i - 1, f, tile(t)] + base[i + 1, f, tile(t)]
    n = n + pltpu.roll(jnp.where(sub == 7, before, c), 1, 0)
    n = n + pltpu.roll(jnp.where(sub == 0, after, c), 7, 0)
    return c, n


def along(c):
    return pltpu.roll(c, 1, 1), pltpu.roll(c, c.shape[1] - 1, 1)


def advance(base, i, t, sub, theta, gain):
    s, ns = around(base, i, 0, t, sub)
    u, nu = around(base, i, 1, t, sub)
    _, nsu = around(base, i, 5, t, sub)
    (s0, s1), (u0, u1) = along(s), along(u)
    ns = ns + s0 + s1
    nu = nu + u0 + u1
    nsu = nsu + s0 * u0 + s1 * u1
    p = base[i, 2, tile(t)]
    g, ng = around(base, i, 3, t, sub)
    sh, nsh = around(base, i, 4, t, sub)
    (g0, g1), (h0, h1) = along(g), along(sh)
    ng = ng + g0 + g1
    nsh = nsh + h0 + h1
    six = 6.0 * s
    phi = 1.0 - s
    hump = 1.0 - phi * phi
    drive = (u + p) + theta
    rise = ((six - ns) + hump * (phi - (hump * drive) * 2.0)) * gain
    flux = (s * nu + nsu) - u * (ns + six)
    source = (DT * DU / 4.0 / HALF) * flux + (0.5 / HALF + u) * rise
    u_new = u + source * pltpu.reciprocal(s + PART / HALF, full_range=False)
    p_new = p + ((s * ng + nsh) - (g * ns + 6.0 * sh))
    return phi, rise, s - rise, u_new, p_new


def fetch(phase, solute, particle, near, sem):
    copies = [
        pltpu.make_async_copy(a.at[pl.ds(0, near.shape[1])], near.at[f], sem.at[f])
        for f, a in enumerate((phase, solute, particle))
    ]
    for c in copies:
        c.start()
    for c in copies:
        c.wait()


def pack(lo, chunks, *refs):
    fields, near, held, refs = refs[:4], refs[4], refs[5:9], refs[9:]
    later, (east, west, sem) = refs[: len(chunks) - 1], refs[len(chunks) - 1 :]
    planes = fields[0].shape[0]
    own, lowest = [], []
    for f in range(3):
        own.append(pltpu.make_async_copy(fields[f].at[pl.ds(lo, planes - lo)], held[f], sem.at[f, 0]))
        first, copies = chunks[0], []
        for k, (part, count) in enumerate(zip(later, chunks[1:])):
            copies.append(pltpu.make_async_copy(fields[f].at[pl.ds(first, count)], part.at[f], sem.at[f, 1 + k]))
            first += count
        lowest.append(copies)
    entering = pltpu.make_async_copy(fields[3], held[3], sem.at[3, 0])
    for f in range(3):
        for c in [own[f], *lowest[f]]:
            c.start()
    entering.start()

    @pl.loop(0, min(lo, chunks[0]))
    def _(i):
        for f in range(3):
            east[f, i] = near[f, i, ROWS - HALO : ROWS]
            west[f, i] = near[f, i, 0:HALO]

    for f in range(3):
        own[f].wait()

        @pl.loop(0, planes - lo)
        def _(i):
            east[f, lo + i] = held[f][i, ROWS - HALO : ROWS]
            west[f, lo + i] = held[f][i, 0:HALO]

    for f in range(3):
        for c in lowest[f]:
            c.wait()
    entering.wait()


def pack_sides(left, right, part, _, done, mixed, __):
    n, t_all = part.shape[1], ROWS // 8

    @pl.loop(0, n)
    def _(i):
        for f in range(3):
            for t in range(t_all):
                mixed[f, t_all * i + t] = part[f, i, tile(t)]

    @pl.loop(0, FAR // 2)
    def _(i):
        for f in range(3):
            rows = [a[f, i + h] for h in (0, FAR // 2) for a in (right, left)]
            mixed[f, t_all * n + i] = jnp.concatenate(rows, axis=0)


N_TILES = ROWS // 8


def planewise(n, tiles):
    step = min(n, max(1, 10 // tiles))

    def over(body):
        whole = n // step * step

        @pl.loop(0, whole, step=step)
        def _(i):
            for k in range(step):
                body(i + k)

        for i in range(whole, n):
            body(jnp.int32(i))

    return over


FULL, INNER, OUTER = "full", "inner", "outer"
MIDDLE_TILES = {FULL: range(TILES), INNER: range(N_TILES), OUTER: (0, N_TILES - 1, TILES - 1)}
FINAL_TILES = {FULL: range(N_TILES), INNER: range(1, N_TILES - 1), OUTER: (0, N_TILES - 1)}


def segment(kind, own, tiled, writes, beside, lo, start, n_new, total, planes, ins, outs, base0, base1, res, out_sem):
    ins = list(ins)
    take = lambda n: [ins.pop(0) for _ in range(n)]
    rows_in = kind != OUTER
    sides_in = kind != INNER
    if own:
        if rows_in:
            fields = take(3)
        if sides_in:
            left, right = take(2)
    else:
        if rows_in:
            (inner,) = take(1)
        if sides_in:
            (mixed,) = take(1)
        (inflow,) = take(1)
    grow = lax.axis_index("grow")
    is_top = grow == lax.axis_size("grow") - 1
    sub = lax.broadcasted_iota(jnp.int32, (8, res.shape[-1]), 0)
    mid0 = start + (1 if own else -1)
    out0 = start + (2 if own else -2)
    n_mid, n_out = (n_new - 2, n_new - 4) if own else (n_new, n_new)
    far0 = start - planes

    @pl.loop(0, n_new)
    def _(i):
        for t in range(N_TILES) if rows_in else ():
            if own:
                phi, u, p = (fields[f][i, tile(t)] for f in range(3))
            elif tiled:
                phi, u, p = (inner[f, N_TILES * i + t] for f in range(3))
            else:
                phi, u, p = (inner[f, i, tile(t)] for f in range(3))
            put(base0, start - lo + i, t, 1.0 - phi, u, p)
        ends = []
        for f in range(3) if sides_in else ():
            if own:
                low, high = left[f, start + i], right[f, start + i]
                ends.append(jnp.concatenate([high, jnp.zeros((4, high.shape[1]), jnp.float32), low], axis=0))
            else:
                upper = far0 + i >= FAR // 2
                both = mixed[f, beside + jnp.where(upper, far0 + i - FAR // 2, far0 + i)]
                ends.append(jnp.where((sub < 4) != upper, both, pltpu.roll(both, 4, 0)))
        if sides_in:
            put(base0, start - lo + i, TILES - 1, 1.0 - ends[0], ends[1], ends[2])

    def close(base, first, at, n):
        if first <= at < first + n:

            @pl.when(is_top)
            def _():
                base[at] = base[at - 1]

    close(base0, start - lo, planes - lo, n_new)

    def coefficients(plane):
        height = (grow * planes + plane).astype(jnp.float32)
        theta = (height - 0.5 * total) / total
        lag = jnp.full(sub.shape, 1.0 - (1.0 - PART) * theta, jnp.float32)
        return theta, DT / lag

    @planewise(n_mid, len(MIDDLE_TILES[kind]))
    def _(i):
        theta, gain = coefficients(mid0 + i)
        for t in MIDDLE_TILES[kind]:
            _, _, s, u, p = advance(base0, mid0 - lo + i, t, sub, theta, gain)
            put(base1, mid0 - lo - 1 + i, t, s, u, p)

    close(base1, mid0 - lo - 1, planes - lo - 1, n_mid)

    def write(i):
        at = out0 - SHIFT + i
        return [pltpu.make_async_copy(res.at[f, at], outs[f].at[at], out_sem.at[f, at]) for f in range(3)]

    @planewise(n_out, len(FINAL_TILES[kind]))
    def _(i):
        theta, gain = coefficients(out0 + i)
        at = out0 - SHIFT + i
        for t in FINAL_TILES[kind]:
            phi, rise, _, u, p = advance(base1, out0 - lo - 1 + i, t, sub, theta, gain)
            res[0, at, tile(t)] = phi + rise
            res[1, at, tile(t)] = u
            res[2, at, tile(t)] = p
        if kind != INNER and not own:

            @pl.when(jnp.logical_and(is_top, out0 + i >= planes))
            def _():
                res[0, at] = jnp.full(res.shape[2:], -1.0, jnp.float32)
                res[1, at] = jnp.full(res.shape[2:], -1.0, jnp.float32)
                res[2, at] = inflow[jnp.maximum(out0 - planes + i, 0)]

        if writes:
            for c in write(i):
                c.start()

    def finish():
        if writes:

            @pl.loop(0, n_out)
            def _(i):
                for c in write(i):
                    c.wait()

    return finish


def several(parts, ready, n_ins, aliased, *refs):
    ins, refs = refs[:n_ins], refs[n_ins + (6 if aliased else 0) :]
    outs, state, sem = refs[:3], refs[3:6], refs[-1]
    if not aliased:
        refs[6][...] = jnp.zeros_like(refs[6])
    copies = []
    if ready:
        first, run_of = ready[0], pl.ds(*ready)
        for f in range(3):
            copies.append(pltpu.make_async_copy(state[2].at[f, run_of], outs[f].at[run_of], sem.at[f, first]))
    for c in copies:
        c.start()
    waits = [part([ins[k] for k in places], outs, *state, sem) for part, places in parts]
    for c in copies:
        c.wait()
    for wait in waits:
        wait()


IN_HBM = pl.BlockSpec(memory_space=pltpu.HBM)
IN_VMEM = pl.BlockSpec(memory_space=pltpu.VMEM)
F32 = jnp.float32


def in_vmem(*shape):
    return pltpu.VMEM(shape, F32)


def near_memory(*arrays):
    return [pltpu.with_memory_space_constraint(a, pltpu.VMEM) for a in arrays]


def run(name, parts, ins, shape, deep, cost, state=None, ready=None):
    planes, rows, ny = shape
    out_shape = [jax.ShapeDtypeStruct(shape, F32)] * 3
    out_shape += [in_vmem(deep, 6, EXT, ny), in_vmem(deep - 2, 6, EXT, ny), in_vmem(3, *shape)]
    args, in_specs, alias = near_memory(*ins), [IN_VMEM] * len(ins), {}
    out_specs = [IN_HBM] * 3 + [IN_VMEM] * 3
    if state is None:
        out_shape.append(in_vmem(8, 128))
        out_specs.append(IN_VMEM)
    else:
        alias = {len(args) + k: k for k in range(6)}
        args += list(state)
        in_specs += [IN_HBM] * 3 + [IN_VMEM] * 3
    return pl.pallas_call(
        functools.partial(several, parts, ready, len(ins), state is not None),
        out_shape=out_shape,
        in_specs=in_specs,
        out_specs=out_specs,
        scratch_shapes=[pltpu.SemaphoreType.DMA((3, planes))],
        input_output_aliases=alias,
        compiler_params=pltpu.CompilerParams(vmem_limit_bytes=4 << 20),
        cost_estimate=pl.CostEstimate(flops=480 * ny * cost, bytes_accessed=128 * ny * cost, transcendentals=0),
        name=name,
    )(*args)


PACK_LIMIT = 57 << 20
CHUNKS = (7, 1, 2)


def on_device(phase, solute, particle, inflow):
    planes, rows, ny = phase.shape
    n_lat, n_grow = lax.axis_size("lat"), lax.axis_size("grow")
    total = float(n_grow * planes)
    down = [(i + 1, i) for i in range(n_grow - 1)]
    to_east = [(i, (i + 1) % n_lat) for i in range(n_lat)]
    to_west = [((i + 1) % n_lat, i) for i in range(n_lat)]
    lo = planes - SHIFT - HALO
    assert CHUNKS[0] >= lo
    fat = pltpu.CompilerParams(vmem_limit_bytes=PACK_LIMIT)
    near = pl.pallas_call(
        fetch,
        out_shape=in_vmem(3, CHUNKS[0], rows, ny),
        in_specs=[IN_HBM] * 3,
        out_specs=IN_VMEM,
        scratch_shapes=[pltpu.SemaphoreType.DMA((3,))],
        compiler_params=fat,
        name="fetch",
    )(phase, solute, particle)
    packed = pl.pallas_call(
        functools.partial(pack, lo, CHUNKS),
        out_shape=[in_vmem(planes - lo, rows, ny)] * 3
        + [in_vmem(*inflow.shape)]
        + [in_vmem(3, n, rows, ny) for n in CHUNKS[1:]]
        + [in_vmem(3, planes, HALO, ny)] * 2,
        in_specs=[IN_HBM] * 4 + [IN_VMEM],
        out_specs=[IN_VMEM] * (5 + len(CHUNKS)),
        scratch_shapes=[pltpu.SemaphoreType.DMA((4, len(CHUNKS)))],
        compiler_params=fat,
        name="pack",
    )(phase, solute, particle, inflow, *near_memory(near))
    fields, inflow, (more, rest), (east, west) = packed[:3], packed[3], packed[4:-2], packed[-2:]
    near = lax.ppermute(near, "grow", down)
    left = lax.ppermute(east, "lat", to_east)
    right = lax.ppermute(west, "lat", to_west)
    beside = CHUNKS[1] * (rows // 8)

    def part(kind, own, tiled, writes, start, n):
        return functools.partial(segment, kind, own, tiled, writes, beside, lo, start, n, total, planes)

    n, start, deep = CHUNKS, planes, planes - lo + FAR
    own = (lo, planes - lo)
    parts = [(part(INNER, True, False, False, *own), (0, 1, 2))]
    *state, done = run("own_inner", parts, fields, phase.shape, deep, 60)
    mixed, rest = pl.pallas_call(
        pack_sides,
        out_shape=[in_vmem(3, beside + FAR // 2, 8, ny), in_vmem(*rest.shape)],
        in_specs=[IN_VMEM] * 5,
        out_specs=[IN_VMEM] * 2,
        input_output_aliases={3: 1},
        compiler_params=pltpu.CompilerParams(vmem_limit_bytes=1 << 20),
        name="pack_sides",
    )(*near_memory(left, right, more, rest, done))
    mixed = lax.ppermute(mixed, "grow", down)
    rest = lax.ppermute(rest, "grow", down)

    parts = [(part(OUTER, True, False, False, *own), (0, 1))]
    state = run("own_outer", parts, (left, right), phase.shape, deep, 50, state)
    parts = [(part(INNER, False, False, False, start, n[0]), (0, 1))]
    n_own = planes - lo - 2 * HALO
    state = run("near_inner", parts, (near, inflow), phase.shape, deep, 60, state, (0, n_own))
    parts = [
        (part(OUTER, False, False, False, start, n[0]), (0, 1)),
        (part(FULL, False, True, False, start + n[0], n[1]), (0, 0, 1)),
    ]
    state = run("near_outer", parts, (mixed, inflow), phase.shape, deep, 60, state)
    parts = [(part(FULL, False, False, True, start + n[0] + n[1], n[2]), (0, 1, 2))]
    state = run("rest", parts, (rest, mixed, inflow), phase.shape, deep, 20, state, (n_own, n[0] + n[1]))
    return tuple(state[:3])


def solution(mesh):
    in_specs = (
        P("grow", "lat", None),
        P("grow", "lat", None),
        P("grow", "lat", None),
        P(None, "lat", None),
    )
    out_specs = (P("grow", "lat", None), P("grow", "lat", None), P("grow", "lat", None))
    return jax.shard_map(
        on_device, mesh=mesh, in_specs=in_specs, out_specs=out_specs, check_vma=False
    )
```
